32 devices in a mesh: az: 8 (over y, x, core), rg: 4 (over z).
Axes of the slice: x: 2, y: 2, z: 4, core: 2. Of those that a mesh axis runs over, the one named last changes fastest.
Arguments:
- raw: bfloat16 [2, 4096, 8192], P(None, 'az', 'rg'), may hold values from -6 to 6
- chirp: bfloat16 [2, 256], replicated, may hold values from -0.25 to 0.25
- az_ref: bfloat16 [2, 64, 512], replicated, may hold values from -0.1875 to 0.1875
- set_index: int32 [8192], P('rg'), may hold values from 0 to 63, as said below
Outputs:
- focused: bfloat16 [2, 4096, 8192], P(None, 'az', 'rg')
The draws below stay inside these ranges and needn't reach their ends.
Inputs may be any that keep to these rules, and one draw needn't show every extreme that they name: `set_index`: range columns come in aligned runs of 256 that share one set index.
All inputs are finite; a program needn't handle non-finite values.
Results may differ from the reference program's by a relative error of at most 0.0049.
Values may be sent and summed in bfloat16 or wider, within the bound.
A program may use at most 64 MiB of HBM per device.

```python
import jax
import jax.numpy as jnp
from jax import lax

KR = 256
KA = 512
SETS = 64
AZ_TOTAL = 4096
RG_TOTAL = 8192
SET_RUN = 256


def draw_set_index(key, part):
    group_count = RG_TOTAL // SET_RUN
    baseline = jnp.arange(group_count, dtype=jnp.int32) * SETS // group_count
    jitter = jax.random.randint(key, (group_count,), -1, 2).astype(jnp.int32)
    values = jnp.clip(baseline + jitter, 0, SETS - 1)
    values = values.at[0].set(0).at[group_count - 1].set(SETS - 1)
    return jnp.repeat(values, SET_RUN).astype(jnp.int32)


def steps_of(own_key, extent, pieces, smallest, top_value):
    def one(axis_at, shards_of):
        steps = jax.random.uniform(jax.random.fold_in(jax.random.fold_in(own_key, 6), axis_at), (shards_of,), jnp.float32, smallest / len(pieces), top_value / len(pieces))
        return jnp.repeat(jnp.exp(steps), extent[axis_at] // shards_of).reshape((-1,) + (1,) * (len(extent) - axis_at - 1))

    factor_of = one(*pieces[0])
    for cut in pieces[1:]:
        factor_of = factor_of * one(*cut)
    return factor_of


def centred(stream_key, dims, spread, limit, pieces=(), kind=jnp.bfloat16):
    array = spread * jax.random.normal(stream_key, dims, jnp.float32)
    if pieces:
        array = array * steps_of(stream_key, dims, pieces, -0.22, 0.18)
    return jnp.clip(array, -limit, limit).astype(kind)


def setup_inputs(seed: int = 0) -> dict:
    splits = jax.random.split(jax.random.key(seed), 5)
    raw = centred(splits[0], (2, AZ_TOTAL, RG_TOTAL), 1.0, 6.0, ((1, 8), (2, 4)))
    chirp = centred(splits[1], (2, KR), (2 * KR) ** -0.5, 0.25)
    az_ref = centred(splits[2], (2, SETS, KA), (2 * KA) ** -0.5, 0.1875)
    set_index = draw_set_index(jax.random.fold_in(splits[4], 71), 0)
    return {"raw": raw, "chirp": chirp, "az_ref": az_ref, "set_index": set_index}


def reference(raw, chirp, az_ref, set_index):
    lines = raw.shape[1]
    columns = raw.shape[2]
    range_taps = chirp.shape[1]
    azimuth_taps = az_ref.shape[2]
    range_len = columns + range_taps
    chirp_c = lax.complex(chirp[0].astype(jnp.float32), chirp[1].astype(jnp.float32))
    chirp_f = jnp.conj(jnp.fft.fft(chirp_c, range_len))
    block_lines = min(512, lines)

    def range_block(segment):
        signal = lax.complex(segment[0].astype(jnp.float32), segment[1].astype(jnp.float32))
        spectrum = jnp.fft.fft(signal, range_len, axis=1) * chirp_f[None, :]
        result = jnp.fft.ifft(spectrum, axis=1)[:, :columns]
        return jnp.stack([jnp.real(result), jnp.imag(result)]).astype(jnp.bfloat16)

    raw_blocks = raw.reshape(2, lines // block_lines, block_lines, columns).transpose(1, 0, 2, 3)
    compressed = lax.map(range_block, raw_blocks).transpose(1, 0, 2, 3).reshape(2, lines, columns)

    azimuth_len = lines + azimuth_taps
    ref_c = lax.complex(az_ref[0].astype(jnp.float32), az_ref[1].astype(jnp.float32))
    ref_f = jnp.conj(jnp.fft.fft(ref_c, azimuth_len, axis=1))
    block_columns = min(512, columns)
    count = columns // block_columns

    def azimuth_block(inputs):
        segment, chosen = inputs
        signal = lax.complex(segment[0].astype(jnp.float32), segment[1].astype(jnp.float32))
        spectrum = jnp.fft.fft(signal, azimuth_len, axis=0) * jnp.take(ref_f, chosen, axis=0).T
        result = jnp.fft.ifft(spectrum, axis=0)[:lines]
        return jnp.stack([jnp.real(result), jnp.imag(result)]).astype(jnp.bfloat16)

    column_blocks = compressed.reshape(2, lines, count, block_columns).transpose(2, 0, 1, 3)
    set_blocks = set_index.reshape(count, block_columns).astype(jnp.int32)
    focused = lax.map(azimuth_block, (column_blocks, set_blocks))
    return focused.transpose(1, 2, 0, 3).reshape(2, lines, columns)
```

```python
import functools

import jax
import jax.numpy as jnp
from jax import lax
from jax.experimental import pallas as pl
from jax.experimental.pallas import tpu as pltpu
from jax.sharding import PartitionSpec as P

MESH = pl.DeviceIdType.MESH


def shifted_rows(row, rows, period):
    padded = jnp.concatenate(
        [row, jnp.zeros((1, period - row.shape[1]), row.dtype)], axis=1
    )
    spread = jnp.broadcast_to(padded, (rows, period))
    return pltpu.roll(spread, 0, 1, stride=1, stride_axis=0)


def kernel(
    az_size, rg_size, run, block,
    raw, chirp, az_ref, set_index, out,
    raw_v, comp, halo, res, range_w, az_w, az_f32,
    in_sem, out_sem, send_sem, recv_sem, edge_sem,
):
    taps = chirp.shape[1]
    az_taps = az_ref.shape[2]
    chunks, _, lines, width = comp.shape
    az, rg = lax.axis_index("az"), lax.axis_index("rg")

    barrier = pltpu.get_barrier_semaphore()
    for axis, me, size in (("az", az, az_size), ("rg", rg, rg_size)):
        for step in (1, size - 1):
            pl.semaphore_signal(
                barrier, inc=1, device_id={axis: lax.rem(me + step, size)},
                device_id_type=MESH,
            )

    def load(chunk):
        start = pl.multiple_of(chunk * width, width)
        return pltpu.make_async_copy(
            raw.at[:, :, pl.ds(start, width)], raw_v.at[chunk], in_sem.at[chunk]
        )

    def store(chunk):
        start = pl.multiple_of(chunk * width, width)
        return pltpu.make_async_copy(
            res.at[chunk], out.at[:, :, pl.ds(start, width)], out_sem.at[chunk]
        )

    def edge():
        return pltpu.make_async_remote_copy(
            src_ref=raw_v.at[0], dst_ref=raw_v.at[chunks],
            send_sem=edge_sem.at[0], recv_sem=edge_sem.at[1],
            device_id={"rg": lax.rem(rg + rg_size - 1, rg_size)}, device_id_type=MESH,
        )

    def send(chunk):
        return pltpu.make_async_remote_copy(
            src_ref=comp.at[chunk], dst_ref=halo.at[chunk],
            send_sem=send_sem.at[chunk], recv_sem=recv_sem.at[chunk],
            device_id={"az": lax.rem(az + az_size - 1, az_size)}, device_id_type=MESH,
        )

    for chunk in range(chunks):
        load(chunk).start()

    for part in range(2):
        row = chirp[pl.ds(part, 1), :].astype(jnp.float32)
        square = shifted_rows(row, width, width + taps)
        range_w[:, part * width:(part + 1) * width] = square.T.astype(jnp.bfloat16)

    az_f32[...] = az_ref[...].astype(jnp.float32)

    @pl.when(rg == rg_size - 1)
    def _():
        raw_v[chunks] = jnp.zeros((2, lines, width), jnp.bfloat16)

    @pl.when(az == az_size - 1)
    def _():
        def clear(chunk, carry):
            halo[chunk] = jnp.zeros((2, lines, width), jnp.bfloat16)
            return carry
        lax.fori_loop(0, chunks, clear, 0)

    load(0).wait()
    pl.semaphore_wait(barrier, 4)

    @pl.when(rg > 0)
    def _():
        edge().start()

    def range_chunk(chunk):
        for first in range(0, lines, block):
            rows = slice(first, first + block)
            real, imag = [
                jnp.dot(raw_v[chunk, part, rows, :], range_w[:width, :],
                        preferred_element_type=jnp.float32)
                + jnp.dot(raw_v[chunk + 1, part, rows, :], range_w[width:, :],
                          preferred_element_type=jnp.float32)
                for part in range(2)
            ]
            comp[chunk, 0, rows, :] = (real[:, :width] + imag[:, width:]).astype(jnp.bfloat16)
            comp[chunk, 1, rows, :] = (imag[:, :width] - real[:, width:]).astype(jnp.bfloat16)

        @pl.when(az > 0)
        def _():
            send(chunk).start()

    def early(chunk, carry):
        load(chunk + 1).wait()
        range_chunk(chunk)
        return carry

    lax.fori_loop(0, chunks - 1, early, 0)

    @pl.when(rg < rg_size - 1)
    def _():
        edge().wait_recv()

    range_chunk(chunks - 1)

    def focus(chunk, carry):
        @pl.when(az < az_size - 1)
        def _():
            send(chunk).wait_recv()

        for first_col in range(0, width, run):
            cols = slice(first_col, first_col + run)
            chosen = set_index[chunk * width + first_col]
            for part in range(2):
                row = az_f32[part, pl.ds(chosen, 1), :]
                square = shifted_rows(row, block, az_taps + 2 * block)
                az_w[part * block:(part + 1) * block, :] = (
                    square[:, :az_taps + block].astype(jnp.bfloat16)
                )
            for first in range(0, lines, block):
                own = min(lines - first, az_taps + block)
                rest = az_taps + block - own
                real, imag = [
                    jnp.dot(az_w[:, :own], comp[chunk, part, first:first + own, cols],
                            preferred_element_type=jnp.float32)
                    + jnp.dot(az_w[:, own:], halo[chunk, part, :rest, cols],
                              preferred_element_type=jnp.float32)
                    for part in range(2)
                ]
                rows = slice(first, first + block)
                res[chunk, 0, rows, cols] = (real[:block] + imag[block:]).astype(jnp.bfloat16)
                res[chunk, 1, rows, cols] = (imag[:block] - real[block:]).astype(jnp.bfloat16)
        store(chunk).start()
        return carry

    lax.fori_loop(0, chunks, focus, 0)

    @pl.when(rg > 0)
    def _():
        edge().wait_send()

    def finish(chunk, carry):
        @pl.when(az > 0)
        def _():
            send(chunk).wait_send()
        store(chunk).wait()
        return carry

    lax.fori_loop(0, chunks, finish, 0)


def local(az_size, rg_size, raw, chirp, az_ref, set_index):
    _, lines, columns = raw.shape
    taps = chirp.shape[1]
    az_taps = az_ref.shape[2]
    width = taps
    chunks = columns // width
    run = min(columns // az_size, width)
    block = az_taps // 2
    assert columns % width == 0 and width % run == 0
    assert lines >= az_taps and lines % block == 0
    halo_shape = (chunks, 2, lines, width)
    return pl.pallas_call(
        functools.partial(kernel, az_size, rg_size, run, block),
        out_shape=jax.ShapeDtypeStruct(raw.shape, jnp.bfloat16),
        in_specs=[
            pl.BlockSpec(memory_space=pl.ANY),
            pl.BlockSpec(memory_space=pltpu.VMEM),
            pl.BlockSpec(memory_space=pltpu.VMEM),
            pl.BlockSpec(memory_space=pltpu.SMEM),
        ],
        out_specs=pl.BlockSpec(memory_space=pl.ANY),
        scratch_shapes=[
            pltpu.VMEM((chunks + 1, 2, lines, width), jnp.bfloat16),
            pltpu.VMEM(halo_shape, jnp.bfloat16),
            pltpu.VMEM(halo_shape, jnp.bfloat16),
            pltpu.VMEM(halo_shape, jnp.bfloat16),
            pltpu.VMEM((width + taps, 2 * width), jnp.bfloat16),
            pltpu.VMEM((2 * block, az_taps + block), jnp.bfloat16),
            pltpu.VMEM(az_ref.shape, jnp.float32),
            pltpu.SemaphoreType.DMA((chunks,)),
            pltpu.SemaphoreType.DMA((chunks,)),
            pltpu.SemaphoreType.DMA((chunks,)),
            pltpu.SemaphoreType.DMA((chunks,)),
            pltpu.SemaphoreType.DMA((2,)),
        ],
        compiler_params=pltpu.CompilerParams(
            collective_id=0, has_side_effects=True, vmem_limit_bytes=40 * 2**20
        ),
        cost_estimate=pl.CostEstimate(
            flops=11 * 10**9, bytes_accessed=4 * raw.size, transcendentals=0
        ),
    )(raw, chirp, az_ref, set_index)


def solution(mesh):
    in_specs = (P(None, "az", "rg"), P(), P(), P("rg"))
    out_specs = P(None, "az", "rg")
    body = functools.partial(local, mesh.shape["az"], mesh.shape["rg"])
    return jax.shard_map(body, mesh=mesh, in_specs=in_specs, out_specs=out_specs, check_vma=False)
```

```python
import functools

import jax
import jax.numpy as jnp
from jax import lax
from jax.experimental import pallas as pl
from jax.experimental.pallas import tpu as pltpu
from jax.sharding import PartitionSpec as P

MESH = pl.DeviceIdType.MESH


def shifted_rows(row, rows, period):
    padded = jnp.concatenate(
        [row, jnp.zeros((1, period - row.shape[1]), row.dtype)], axis=1
    )
    spread = jnp.broadcast_to(padded, (rows, period))
    return pltpu.roll(spread, 0, 1, stride=1, stride_axis=0)


def kernel(
    az_size, rg_size, run,
    raw, chirp, az_ref, set_index, out,
    raw_v, comp, halo, res, range_w, az_w, sums, chirp_v, az_v, az_f32, sets,
    in_sem, out_sem, send_sem, recv_sem, edge_sem, small_sem,
):
    taps = chirp.shape[1]
    chunks, own_blocks, _, block, width = comp.shape
    halo_blocks = halo.shape[1]
    az, rg = lax.axis_index("az"), lax.axis_index("rg")

    barrier = pltpu.get_barrier_semaphore()
    for axis, me, size in (("az", az, az_size), ("rg", rg, rg_size)):
        for step in (1, size - 1):
            pl.semaphore_signal(
                barrier, inc=1, device_id={axis: lax.rem(me + step, size)},
                device_id_type=MESH,
            )

    def load(chunk):
        start = pl.multiple_of(chunk * width, width)
        return pltpu.make_async_copy(
            raw.at[:, :, pl.ds(start, width)], raw_v.at[chunk], in_sem.at[chunk]
        )

    def store(chunk, part):
        start = pl.multiple_of(chunk * width, width)
        return pltpu.make_async_copy(
            res.at[chunk, part],
            out.at[:, part * block:(part + 1) * block, pl.ds(start, width)],
            out_sem.at[chunk, part],
        )

    def edge():
        return pltpu.make_async_remote_copy(
            src_ref=raw_v.at[0], dst_ref=raw_v.at[chunks],
            send_sem=edge_sem.at[0], recv_sem=edge_sem.at[1],
            device_id={"rg": lax.rem(rg + rg_size - 1, rg_size)}, device_id_type=MESH,
        )

    def send(chunk, part):
        return pltpu.make_async_remote_copy(
            src_ref=comp.at[chunk, part], dst_ref=halo.at[chunk, part],
            send_sem=send_sem.at[chunk, part], recv_sem=recv_sem.at[chunk, part],
            device_id={"az": lax.rem(az + az_size - 1, az_size)}, device_id_type=MESH,
        )

    chirp_load = pltpu.make_async_copy(chirp, chirp_v, small_sem.at[0])
    az_load = pltpu.make_async_copy(az_ref, az_v, small_sem.at[1])
    sets_load = pltpu.make_async_copy(set_index, sets, small_sem.at[2])
    chirp_load.start()
    for chunk in range(chunks):
        load(chunk).start()
    az_load.start()
    sets_load.start()

    chirp_load.wait()
    for part in range(2):
        row = chirp_v[pl.ds(part, 1), :].astype(jnp.float32)
        square = shifted_rows(row, width, width + taps)
        range_w[:, part * width:(part + 1) * width] = square.T.astype(jnp.bfloat16)

    load(0).wait()
    pl.semaphore_wait(barrier, 4)

    @pl.when(rg > 0)
    def _():
        edge().start()

    @pl.when(rg == rg_size - 1)
    def _():
        raw_v[chunks] = jnp.zeros(raw_v.shape[1:], jnp.bfloat16)

    def range_chunk(chunk):
        for part in range(own_blocks):
            rows = slice(part * block, (part + 1) * block)
            real, imag = [
                jnp.dot(raw_v[chunk, side, rows, :], range_w[:width, :],
                        preferred_element_type=jnp.float32)
                + jnp.dot(raw_v[chunk + 1, side, rows, :], range_w[width:, :],
                          preferred_element_type=jnp.float32)
                for side in range(2)
            ]
            comp[chunk, part, 0] = (real[:, :width] + imag[:, width:]).astype(jnp.bfloat16)
            comp[chunk, part, 1] = (imag[:, :width] - real[:, width:]).astype(jnp.bfloat16)

            if part < halo_blocks:
                @pl.when(az > 0)
                def _():
                    send(chunk, part).start()

    def early(chunk, carry):
        load(chunk + 1).wait()
        range_chunk(chunk)
        return carry

    lax.fori_loop(0, chunks - 1, early, 0)

    az_load.wait()
    sets_load.wait()
    az_f32[...] = az_v[...].astype(jnp.float32)

    @pl.when(az == az_size - 1)
    def _():
        def clear(chunk, carry):
            halo[chunk] = jnp.zeros(halo.shape[1:], jnp.bfloat16)
            return carry
        lax.fori_loop(0, chunks, clear, 0)

    @pl.when(rg < rg_size - 1)
    def _():
        edge().wait_recv()

    range_chunk(chunks - 1)

    def product(first_col, shift, values):
        return jnp.dot(
            az_w[first_col // run, :, shift * block:(shift + 1) * block], values,
            preferred_element_type=jnp.float32,
        )

    def focus(chunk, carry):
        for first_col in range(0, width, run):
            cols = slice(first_col, first_col + run)
            chosen = sets[chunk * width + first_col]
            for side in range(2):
                row = az_f32[side, pl.ds(chosen, 1), :]
                square = shifted_rows(row, block, (halo_blocks + 2) * block)
                az_w[first_col // run, side * block:(side + 1) * block, :] = (
                    square[:, :(halo_blocks + 1) * block].astype(jnp.bfloat16)
                )
            for part in range(own_blocks):
                for side in range(2):
                    sums[part, side, :, cols] = sum(
                        product(first_col, shift, comp[chunk, part + shift, side, :, cols])
                        for shift in range(min(halo_blocks + 1, own_blocks - part))
                    )

        for landed in range(-1, halo_blocks):
            if landed >= 0:
                @pl.when(az < az_size - 1)
                def _():
                    send(chunk, landed).wait_recv()

            for part in range(own_blocks):
                shift = own_blocks + landed - part
                last = shift == halo_blocks
                if landed < 0 and not last or shift > halo_blocks:
                    continue
                for first_col in range(0, width, run):
                    cols = slice(first_col, first_col + run)
                    total = [
                        sums[part, side, :, cols]
                        if landed < 0
                        else sums[part, side, :, cols]
                        + product(first_col, shift, halo[chunk, landed, side, :, cols])
                        for side in range(2)
                    ]
                    if last:
                        real, imag = total
                        res[chunk, part, 0, :, cols] = (
                            real[:block] + imag[block:]
                        ).astype(jnp.bfloat16)
                        res[chunk, part, 1, :, cols] = (
                            imag[:block] - real[block:]
                        ).astype(jnp.bfloat16)
                    else:
                        for side in range(2):
                            sums[part, side, :, cols] = total[side]
                if last:
                    store(chunk, part).start()
        return carry

    lax.fori_loop(0, chunks, focus, 0)

    @pl.when(rg > 0)
    def _():
        edge().wait_send()

    def finish(chunk, carry):
        for part in range(halo_blocks):
            @pl.when(az > 0)
            def _():
                send(chunk, part).wait_send()

        for part in range(own_blocks):
            store(chunk, part).wait()
        return carry

    lax.fori_loop(0, chunks, finish, 0)


def local(az_size, rg_size, raw, chirp, az_ref, set_index):
    _, lines, columns = raw.shape
    taps = chirp.shape[1]
    az_taps = az_ref.shape[2]
    width = taps
    chunks = columns // width
    run = min(columns // az_size, width)
    block = az_taps // 2
    own_blocks, halo_blocks = lines // block, az_taps // block
    assert columns % width == 0 and width % run == 0
    assert lines % block == 0 and own_blocks == halo_blocks
    tile = (2, block, width)
    return pl.pallas_call(
        functools.partial(kernel, az_size, rg_size, run),
        out_shape=jax.ShapeDtypeStruct(raw.shape, jnp.bfloat16),
        in_specs=[pl.BlockSpec(memory_space=pltpu.HBM)] * 4,
        out_specs=pl.BlockSpec(memory_space=pl.ANY),
        scratch_shapes=[
            pltpu.VMEM((chunks + 1, 2, lines, width), jnp.bfloat16),
            pltpu.VMEM((chunks, own_blocks) + tile, jnp.bfloat16),
            pltpu.VMEM((chunks, halo_blocks) + tile, jnp.bfloat16),
            pltpu.VMEM((chunks, own_blocks) + tile, jnp.bfloat16),
            pltpu.VMEM((width + taps, 2 * width), jnp.bfloat16),
            pltpu.VMEM((width // run, 2 * block, (halo_blocks + 1) * block), jnp.bfloat16),
            pltpu.VMEM((own_blocks, 2, 2 * block, width), jnp.float32),
            pltpu.VMEM(chirp.shape, chirp.dtype),
            pltpu.VMEM(az_ref.shape, az_ref.dtype),
            pltpu.VMEM(az_ref.shape, jnp.float32),
            pltpu.SMEM(set_index.shape, set_index.dtype),
            pltpu.SemaphoreType.DMA((chunks,)),
            pltpu.SemaphoreType.DMA((chunks, own_blocks)),
            pltpu.SemaphoreType.DMA((chunks, halo_blocks)),
            pltpu.SemaphoreType.DMA((chunks, halo_blocks)),
            pltpu.SemaphoreType.DMA((2,)),
            pltpu.SemaphoreType.DMA((3,)),
        ],
        compiler_params=pltpu.CompilerParams(
            collective_id=0, has_side_effects=True, vmem_limit_bytes=60 * 2**20
        ),
        cost_estimate=pl.CostEstimate(
            flops=11 * 10**9, bytes_accessed=4 * raw.size, transcendentals=0
        ),
    )(raw, chirp, az_ref, set_index)


def solution(mesh):
    in_specs = (P(None, "az", "rg"), P(), P(), P("rg"))
    out_specs = P(None, "az", "rg")
    body = functools.partial(local, mesh.shape["az"], mesh.shape["rg"])
    return jax.shard_map(body, mesh=mesh, in_specs=in_specs, out_specs=out_specs, check_vma=False)
```

```python
import functools

import jax
import jax.numpy as jnp
from jax import lax
from jax.experimental import pallas as pl
from jax.experimental.pallas import tpu as pltpu
from jax.sharding import PartitionSpec as P

MESH = pl.DeviceIdType.MESH


def shifted_rows(row, rows, period):
    padded = jnp.concatenate(
        [row, jnp.zeros((1, period - row.shape[1]), row.dtype)], axis=1
    )
    spread = jnp.broadcast_to(padded, (rows, period))
    return pltpu.roll(spread, 0, 1, stride=1, stride_axis=0)


def kernel(
    az_size, rg_size, run,
    raw, chirp, az_ref, set_index, out,
    raw_v, comp, halo, range_w, az_w, sums, chirp_v, az_v, az_f32, sets,
    in_sem, send_sem, recv_sem, edge_sem, small_sem,
):
    taps = chirp.shape[1]
    chunks, own_blocks, _, block, width = comp.shape
    halo_blocks = halo.shape[1]
    az, rg = lax.axis_index("az"), lax.axis_index("rg")

    barrier = pltpu.get_barrier_semaphore()
    for axis, me, size in (("az", az, az_size), ("rg", rg, rg_size)):
        for step in (1, size - 1):
            pl.semaphore_signal(
                barrier, inc=1, device_id={axis: lax.rem(me + step, size)},
                device_id_type=MESH,
            )

    def load(chunk):
        start = pl.multiple_of(chunk * width, width)
        return pltpu.make_async_copy(
            raw.at[:, :, pl.ds(start, width)], raw_v.at[chunk], in_sem.at[chunk]
        )

    def edge():
        return pltpu.make_async_remote_copy(
            src_ref=raw_v.at[0], dst_ref=raw_v.at[chunks],
            send_sem=edge_sem.at[0], recv_sem=edge_sem.at[1],
            device_id={"rg": lax.rem(rg + rg_size - 1, rg_size)}, device_id_type=MESH,
        )

    def send(chunk, part):
        return pltpu.make_async_remote_copy(
            src_ref=comp.at[chunk, part], dst_ref=halo.at[chunk, part],
            send_sem=send_sem.at[chunk, part], recv_sem=recv_sem.at[chunk, part],
            device_id={"az": lax.rem(az + az_size - 1, az_size)}, device_id_type=MESH,
        )

    chirp_load = pltpu.make_async_copy(chirp, chirp_v, small_sem.at[0])
    az_load = pltpu.make_async_copy(az_ref, az_v, small_sem.at[1])
    sets_load = pltpu.make_async_copy(set_index, sets, small_sem.at[2])
    chirp_load.start()
    for chunk in range(chunks):
        load(chunk).start()
    az_load.start()
    sets_load.start()

    chirp_load.wait()
    for part in range(2):
        row = chirp_v[pl.ds(part, 1), :].astype(jnp.float32)
        square = shifted_rows(row, width, width + taps)
        range_w[:, part * width:(part + 1) * width] = square.T.astype(jnp.bfloat16)

    load(0).wait()
    pl.semaphore_wait(barrier, 4)

    @pl.when(rg > 0)
    def _():
        edge().start()

    @pl.when(rg == rg_size - 1)
    def _():
        raw_v[chunks] = jnp.zeros(raw_v.shape[1:], jnp.bfloat16)

    def range_chunk(chunk):
        for part in range(own_blocks):
            rows = slice(part * block, (part + 1) * block)
            real, imag = [
                jnp.dot(raw_v[chunk, side, rows, :], range_w[:width, :],
                        preferred_element_type=jnp.float32)
                + jnp.dot(raw_v[chunk + 1, side, rows, :], range_w[width:, :],
                          preferred_element_type=jnp.float32)
                for side in range(2)
            ]
            comp[chunk, part, 0] = (real[:, :width] + imag[:, width:]).astype(jnp.bfloat16)
            comp[chunk, part, 1] = (imag[:, :width] - real[:, width:]).astype(jnp.bfloat16)

            if part < halo_blocks:
                @pl.when(az > 0)
                def _():
                    send(chunk, part).start()

    def early(chunk, carry):
        load(chunk + 1).wait()
        range_chunk(chunk)
        return carry

    lax.fori_loop(0, chunks - 1, early, 0)

    az_load.wait()
    sets_load.wait()
    az_f32[...] = az_v[...].astype(jnp.float32)

    @pl.when(az == az_size - 1)
    def _():
        def clear(chunk, carry):
            halo[chunk] = jnp.zeros(halo.shape[1:], jnp.bfloat16)
            return carry
        lax.fori_loop(0, chunks, clear, 0)

    @pl.when(rg < rg_size - 1)
    def _():
        edge().wait_recv()

    range_chunk(chunks - 1)

    def product(first_col, shift, values):
        return jnp.dot(
            az_w[first_col // run, :, shift * block:(shift + 1) * block], values,
            preferred_element_type=jnp.float32,
        )

    def focus(chunk, carry):
        for first_col in range(0, width, run):
            cols = slice(first_col, first_col + run)
            chosen = sets[chunk * width + first_col]
            for side in range(2):
                row = az_f32[side, pl.ds(chosen, 1), :]
                square = shifted_rows(row, block, (halo_blocks + 2) * block)
                az_w[first_col // run, side * block:(side + 1) * block, :] = (
                    square[:, :(halo_blocks + 1) * block].astype(jnp.bfloat16)
                )
            for part in range(own_blocks):
                for side in range(2):
                    sums[part, side, :, cols] = sum(
                        product(first_col, shift, comp[chunk, part + shift, side, :, cols])
                        for shift in range(min(halo_blocks + 1, own_blocks - part))
                    )

        for landed in range(-1, halo_blocks):
            if landed >= 0:
                @pl.when(az < az_size - 1)
                def _():
                    send(chunk, landed).wait_recv()

            for part in range(own_blocks):
                shift = own_blocks + landed - part
                last = shift == halo_blocks
                if landed < 0 and not last or shift > halo_blocks:
                    continue
                for first_col in range(0, width, run):
                    cols = slice(first_col, first_col + run)
                    total = [
                        sums[part, side, :, cols]
                        if landed < 0
                        else sums[part, side, :, cols]
                        + product(first_col, shift, halo[chunk, landed, side, :, cols])
                        for side in range(2)
                    ]
                    if last:
                        real, imag = total
                        rows = slice(part * block, (part + 1) * block)
                        start = pl.multiple_of(chunk * width + first_col, run)
                        out[0, rows, pl.ds(start, run)] = (
                            real[:block] + imag[block:]
                        ).astype(jnp.bfloat16)
                        out[1, rows, pl.ds(start, run)] = (
                            imag[:block] - real[block:]
                        ).astype(jnp.bfloat16)
                    else:
                        for side in range(2):
                            sums[part, side, :, cols] = total[side]
        return carry

    lax.fori_loop(0, chunks, focus, 0)

    @pl.when(rg > 0)
    def _():
        edge().wait_send()

    def finish(chunk, carry):
        for part in range(halo_blocks):
            @pl.when(az > 0)
            def _():
                send(chunk, part).wait_send()
        return carry

    lax.fori_loop(0, chunks, finish, 0)


def local(az_size, rg_size, raw, chirp, az_ref, set_index):
    _, lines, columns = raw.shape
    taps = chirp.shape[1]
    az_taps = az_ref.shape[2]
    width = taps
    chunks = columns // width
    run = min(columns // az_size, width)
    block = az_taps // 2
    own_blocks, halo_blocks = lines // block, az_taps // block
    assert columns % width == 0 and width % run == 0
    assert lines % block == 0 and own_blocks == halo_blocks
    tile = (2, block, width)
    return pl.pallas_call(
        functools.partial(kernel, az_size, rg_size, run),
        out_shape=pltpu.VMEM(raw.shape, jnp.bfloat16),
        in_specs=[pl.BlockSpec(memory_space=pl.ANY)] * 4,
        out_specs=pl.BlockSpec(memory_space=pltpu.VMEM),
        scratch_shapes=[
            pltpu.VMEM((chunks + 1, 2, lines, width), jnp.bfloat16),
            pltpu.VMEM((chunks, own_blocks) + tile, jnp.bfloat16),
            pltpu.VMEM((chunks, halo_blocks) + tile, jnp.bfloat16),
            pltpu.VMEM((width + taps, 2 * width), jnp.bfloat16),
            pltpu.VMEM((width // run, 2 * block, (halo_blocks + 1) * block), jnp.bfloat16),
            pltpu.VMEM((own_blocks, 2, 2 * block, width), jnp.float32),
            pltpu.VMEM(chirp.shape, chirp.dtype),
            pltpu.VMEM(az_ref.shape, az_ref.dtype),
            pltpu.VMEM(az_ref.shape, jnp.float32),
            pltpu.SMEM(set_index.shape, set_index.dtype),
            pltpu.SemaphoreType.DMA((chunks,)),
            pltpu.SemaphoreType.DMA((chunks, halo_blocks)),
            pltpu.SemaphoreType.DMA((chunks, halo_blocks)),
            pltpu.SemaphoreType.DMA((2,)),
            pltpu.SemaphoreType.DMA((3,)),
        ],
        compiler_params=pltpu.CompilerParams(
            collective_id=0, has_side_effects=True, vmem_limit_bytes=56 * 2**20
        ),
        cost_estimate=pl.CostEstimate(
            flops=11 * 10**9, bytes_accessed=4 * raw.size, transcendentals=0
        ),
    )(raw, chirp, az_ref, set_index)


def solution(mesh):
    in_specs = (P(None, "az", "rg"), P(), P(), P("rg"))
    out_specs = P(None, "az", "rg")
    body = functools.partial(local, mesh.shape["az"], mesh.shape["rg"])
    return jax.shard_map(body, mesh=mesh, in_specs=in_specs, out_specs=out_specs, check_vma=False)
```

```python
import functools

import jax
import jax.numpy as jnp
from jax import lax
from jax.experimental import pallas as pl
from jax.experimental.pallas import tpu as pltpu
from jax.sharding import PartitionSpec as P

MESH = pl.DeviceIdType.MESH


def shifted_rows(row, rows, period):
    padded = row
    if row.shape[1] < period:
        padded = jnp.concatenate(
            [row, jnp.zeros((1, period - row.shape[1]), row.dtype)], axis=1
        )
    spread = jnp.broadcast_to(padded, (rows, period))
    return pltpu.roll(spread, 0, 1, stride=1, stride_axis=0)


def kernel(
    az_size, rg_size, run,
    raw, chirp, az_ref, set_index, out,
    raw_v, comp, halo, range_w, az_w, sums, chirp_v, az_v, az_f32, sets,
    in_sem, send_sem, recv_sem, edge_sem, small_sem,
):
    taps = chirp.shape[1]
    chunks, own_blocks, _, block, width = comp.shape
    halo_blocks = halo.shape[1]
    az, rg = lax.axis_index("az"), lax.axis_index("rg")

    barrier = pltpu.get_barrier_semaphore()
    for axis, me, size in (("az", az, az_size), ("rg", rg, rg_size)):
        for step in (1, size - 1):
            pl.semaphore_signal(
                barrier, inc=1, device_id={axis: lax.rem(me + step, size)},
                device_id_type=MESH,
            )

    def load(chunk):
        start = pl.multiple_of(chunk * width, width)
        return pltpu.make_async_copy(
            raw.at[:, :, pl.ds(start, width)], raw_v.at[chunk], in_sem.at[chunk]
        )

    def start_load(chunk, carry):
        load(chunk).start()
        return carry

    def edge():
        return pltpu.make_async_remote_copy(
            src_ref=raw_v.at[0], dst_ref=raw_v.at[chunks],
            send_sem=edge_sem.at[0], recv_sem=edge_sem.at[1],
            device_id={"rg": lax.rem(rg + rg_size - 1, rg_size)}, device_id_type=MESH,
        )

    def send(chunk, part):
        return pltpu.make_async_remote_copy(
            src_ref=comp.at[chunk, part], dst_ref=halo.at[chunk, part],
            send_sem=send_sem.at[chunk, part], recv_sem=recv_sem.at[chunk, part],
            device_id={"az": lax.rem(az + az_size - 1, az_size)}, device_id_type=MESH,
        )

    chirp_load = pltpu.make_async_copy(chirp, chirp_v, small_sem.at[0])
    az_load = pltpu.make_async_copy(az_ref, az_v, small_sem.at[1])
    sets_load = pltpu.make_async_copy(set_index, sets, small_sem.at[2])
    chirp_load.start()
    load(0).start()
    load(1).start()

    circle = width + taps
    total = lax.broadcasted_iota(jnp.int32, (taps, circle), 0) + lax.broadcasted_iota(
        jnp.int32, (taps, circle), 1
    )
    reverse = ((total == 0) | (total == circle)).astype(jnp.bfloat16)
    chirp_load.wait()
    reversed_rows = jnp.dot(chirp_v[...], reverse, preferred_element_type=jnp.float32)
    for side in range(2):
        weights = shifted_rows(reversed_rows[side:side + 1], taps, circle).astype(jnp.bfloat16)
        cols = slice(side * width, (side + 1) * width)
        range_w[:taps, cols] = weights[:, :width]
        range_w[taps:, cols] = weights[:, width:]

    load(0).wait()
    pl.semaphore_wait(barrier, 4)
    lax.fori_loop(2, chunks, start_load, 0)
    az_load.start()
    sets_load.start()

    @pl.when(rg > 0)
    def _():
        edge().start()

    def range_chunk(chunk):
        for part in range(own_blocks):
            rows = slice(part * block, (part + 1) * block)
            real, imag = [
                jnp.dot(raw_v[chunk, side, rows, :], range_w[:width, :],
                        preferred_element_type=jnp.float32)
                + jnp.dot(raw_v[chunk + 1, side, rows, :], range_w[width:, :],
                          preferred_element_type=jnp.float32)
                for side in range(2)
            ]
            comp[chunk, part, 0] = (real[:, :width] + imag[:, width:]).astype(jnp.bfloat16)
            comp[chunk, part, 1] = (imag[:, :width] - real[:, width:]).astype(jnp.bfloat16)

            if part < halo_blocks:
                @pl.when(az > 0)
                def _():
                    send(chunk, part).start()

    def early(chunk, carry):
        load(chunk + 1).wait()
        range_chunk(chunk)
        return carry

    lax.fori_loop(0, chunks - 1, early, 0)

    az_load.wait()
    sets_load.wait()
    az_f32[...] = az_v[...].astype(jnp.float32)

    @pl.when(az == az_size - 1)
    def _():
        def clear(chunk, carry):
            halo[chunk] = jnp.zeros(halo.shape[1:], jnp.bfloat16)
            return carry
        lax.fori_loop(0, chunks, clear, 0)

    @pl.when(rg == rg_size - 1)
    def _():
        raw_v[chunks] = jnp.zeros(raw_v.shape[1:], jnp.bfloat16)

    @pl.when(rg < rg_size - 1)
    def _():
        edge().wait_recv()

    range_chunk(chunks - 1)

    def product(first_col, shift, values):
        return jnp.dot(
            az_w[first_col // run, :, shift * block:(shift + 1) * block], values,
            preferred_element_type=jnp.float32,
        )

    def focus(chunk, carry):
        for first_col in range(0, width, run):
            cols = slice(first_col, first_col + run)
            chosen = sets[chunk * width + first_col]
            for side in range(2):
                row = az_f32[side, pl.ds(chosen, 1), :]
                square = shifted_rows(row, block, (halo_blocks + 2) * block)
                az_w[first_col // run, side * block:(side + 1) * block, :] = (
                    square[:, :(halo_blocks + 1) * block].astype(jnp.bfloat16)
                )
            for part in range(own_blocks):
                for side in range(2):
                    sums[part, side, :, cols] = sum(
                        product(first_col, shift, comp[chunk, part + shift, side, :, cols])
                        for shift in range(min(halo_blocks + 1, own_blocks - part))
                    )

        for landed in range(-1, halo_blocks):
            if landed >= 0:
                @pl.when(az < az_size - 1)
                def _():
                    send(chunk, landed).wait_recv()

            for part in range(own_blocks):
                shift = own_blocks + landed - part
                last = shift == halo_blocks
                if landed < 0 and not last or shift > halo_blocks:
                    continue
                for first_col in range(0, width, run):
                    cols = slice(first_col, first_col + run)
                    total = [
                        sums[part, side, :, cols]
                        if landed < 0
                        else sums[part, side, :, cols]
                        + product(first_col, shift, halo[chunk, landed, side, :, cols])
                        for side in range(2)
                    ]
                    if last:
                        real, imag = total
                        rows = slice(part * block, (part + 1) * block)
                        start = pl.multiple_of(chunk * width + first_col, run)
                        out[0, rows, pl.ds(start, run)] = (
                            real[:block] + imag[block:]
                        ).astype(jnp.bfloat16)
                        out[1, rows, pl.ds(start, run)] = (
                            imag[:block] - real[block:]
                        ).astype(jnp.bfloat16)
                    else:
                        for side in range(2):
                            sums[part, side, :, cols] = total[side]
        return carry

    lax.fori_loop(0, chunks, focus, 0)

    @pl.when(rg > 0)
    def _():
        edge().wait_send()

    def finish(chunk, carry):
        for part in range(halo_blocks):
            @pl.when(az > 0)
            def _():
                send(chunk, part).wait_send()
        return carry

    lax.fori_loop(0, chunks, finish, 0)


def local(az_size, rg_size, raw, chirp, az_ref, set_index):
    _, lines, columns = raw.shape
    taps = chirp.shape[1]
    az_taps = az_ref.shape[2]
    width = taps
    chunks = columns // width
    run = min(columns // az_size, width)
    block = az_taps // 2
    own_blocks, halo_blocks = lines // block, az_taps // block
    assert columns % width == 0 and width % run == 0 and chunks > 1
    assert lines % block == 0 and own_blocks == halo_blocks
    tile = (2, block, width)
    return pl.pallas_call(
        functools.partial(kernel, az_size, rg_size, run),
        out_shape=pltpu.VMEM(raw.shape, jnp.bfloat16),
        in_specs=[pl.BlockSpec(memory_space=pl.ANY)] * 4,
        out_specs=pl.BlockSpec(memory_space=pltpu.VMEM),
        scratch_shapes=[
            pltpu.VMEM((chunks + 1, 2, lines, width), jnp.bfloat16),
            pltpu.VMEM((chunks, own_blocks) + tile, jnp.bfloat16),
            pltpu.VMEM((chunks, halo_blocks) + tile, jnp.bfloat16),
            pltpu.VMEM((width + taps, 2 * width), jnp.bfloat16),
            pltpu.VMEM((width // run, 2 * block, (halo_blocks + 1) * block), jnp.bfloat16),
            pltpu.VMEM((own_blocks, 2, 2 * block, width), jnp.float32),
            pltpu.VMEM(chirp.shape, chirp.dtype),
            pltpu.VMEM(az_ref.shape, az_ref.dtype),
            pltpu.VMEM(az_ref.shape, jnp.float32),
            pltpu.SMEM(set_index.shape, set_index.dtype),
            pltpu.SemaphoreType.DMA((chunks,)),
            pltpu.SemaphoreType.DMA((chunks, halo_blocks)),
            pltpu.SemaphoreType.DMA((chunks, halo_blocks)),
            pltpu.SemaphoreType.DMA((2,)),
            pltpu.SemaphoreType.DMA((3,)),
        ],
        compiler_params=pltpu.CompilerParams(
            collective_id=0, has_side_effects=True, vmem_limit_bytes=56 * 2**20
        ),
        cost_estimate=pl.CostEstimate(
            flops=11 * 10**9, bytes_accessed=4 * raw.size, transcendentals=0
        ),
    )(raw, chirp, az_ref, set_index)


def solution(mesh):
    in_specs = (P(None, "az", "rg"), P(), P(), P("rg"))
    out_specs = P(None, "az", "rg")
    body = functools.partial(local, mesh.shape["az"], mesh.shape["rg"])
    return jax.shard_map(body, mesh=mesh, in_specs=in_specs, out_specs=out_specs, check_vma=False)
```

```python
import functools

import jax
import jax.numpy as jnp
from jax import lax
from jax.experimental import pallas as pl
from jax.experimental.pallas import tpu as pltpu
from jax.sharding import PartitionSpec as P

MESH = pl.DeviceIdType.MESH


def shifted_rows(row, rows, period):
    padded = row
    if row.shape[1] < period:
        padded = jnp.concatenate(
            [row, jnp.zeros((1, period - row.shape[1]), row.dtype)], axis=1
        )
    spread = jnp.broadcast_to(padded, (rows, period))
    return pltpu.roll(spread, 0, 1, stride=1, stride_axis=0)


def kernel(
    az_size, rg_size, run,
    raw, chirp, az_ref, set_index, out,
    raw_v, comp, halo, range_w, az_w, sums, chirp_v, az_v, az_f32, sets,
    in_sem, send_sem, recv_sem, edge_sem, small_sem,
):
    taps = chirp.shape[1]
    chunks, own_blocks, _, block, width = comp.shape
    halo_blocks = halo.shape[1]
    az, rg = lax.axis_index("az"), lax.axis_index("rg")

    barrier = pltpu.get_barrier_semaphore()
    for axis, me, size in (("az", az, az_size), ("rg", rg, rg_size)):
        for step in (1, size - 1):
            pl.semaphore_signal(
                barrier, inc=1, device_id={axis: lax.rem(me + step, size)},
                device_id_type=MESH,
            )

    def load(chunk):
        start = pl.multiple_of(chunk * width, width)
        return pltpu.make_async_copy(
            raw.at[:, :, pl.ds(start, width)], raw_v.at[chunk], in_sem.at[chunk]
        )

    def start_load(chunk, carry):
        load(chunk).start()
        return carry

    def edge():
        return pltpu.make_async_remote_copy(
            src_ref=raw_v.at[0], dst_ref=raw_v.at[chunks],
            send_sem=edge_sem.at[0], recv_sem=edge_sem.at[1],
            device_id={"rg": lax.rem(rg + rg_size - 1, rg_size)}, device_id_type=MESH,
        )

    def send(chunk, part):
        return pltpu.make_async_remote_copy(
            src_ref=comp.at[chunk, part], dst_ref=halo.at[chunk, part],
            send_sem=send_sem.at[chunk, part], recv_sem=recv_sem.at[chunk, part],
            device_id={"az": lax.rem(az + az_size - 1, az_size)}, device_id_type=MESH,
        )

    chirp_load = pltpu.make_async_copy(chirp, chirp_v, small_sem.at[0])
    az_load = pltpu.make_async_copy(az_ref, az_v, small_sem.at[1])
    sets_load = pltpu.make_async_copy(set_index, sets, small_sem.at[2])
    chirp_load.start()
    load(0).start()
    load(1).start()

    circle = width + taps
    total = lax.broadcasted_iota(jnp.int32, (taps, circle), 0) + lax.broadcasted_iota(
        jnp.int32, (taps, circle), 1
    )
    reverse = ((total == 0) | (total == circle)).astype(jnp.bfloat16)
    chirp_load.wait()
    reversed_rows = jnp.dot(chirp_v[...], reverse, preferred_element_type=jnp.float32)
    for side in range(2):
        weights = shifted_rows(reversed_rows[side:side + 1], taps, circle).astype(jnp.bfloat16)
        cols = slice(side * width, (side + 1) * width)
        range_w[:taps, cols] = weights[:, :width]
        range_w[taps:, cols] = weights[:, width:]

    load(0).wait()
    pl.semaphore_wait(barrier, 4)
    lax.fori_loop(2, chunks, start_load, 0)
    az_load.start()
    sets_load.start()

    @pl.when(rg > 0)
    def _():
        edge().start()

    def range_chunk(chunk):
        for part in range(own_blocks):
            rows = slice(part * block, (part + 1) * block)
            real, imag = [
                jnp.dot(raw_v[chunk, side, rows, :], range_w[:width, :],
                        preferred_element_type=jnp.float32)
                + jnp.dot(raw_v[chunk + 1, side, rows, :], range_w[width:, :],
                          preferred_element_type=jnp.float32)
                for side in range(2)
            ]
            comp[chunk, part, 0] = (real[:, :width] + imag[:, width:]).astype(jnp.bfloat16)
            comp[chunk, part, 1] = (imag[:, :width] - real[:, width:]).astype(jnp.bfloat16)

            if part < halo_blocks:
                @pl.when(az > 0)
                def _():
                    send(chunk, part).start()

    def early(chunk, carry):
        load(chunk + 1).wait()
        range_chunk(chunk)
        return carry

    lax.fori_loop(0, chunks - 1, early, 0)

    az_load.wait()
    sets_load.wait()
    az_f32[...] = az_v[...].astype(jnp.float32)

    @pl.when(az == az_size - 1)
    def _():
        def clear(chunk, carry):
            halo[chunk] = jnp.zeros(halo.shape[1:], jnp.bfloat16)
            return carry
        lax.fori_loop(0, chunks, clear, 0)

    @pl.when(rg == rg_size - 1)
    def _():
        raw_v[chunks] = jnp.zeros(raw_v.shape[1:], jnp.bfloat16)

    @pl.when(rg < rg_size - 1)
    def _():
        edge().wait_recv()

    range_chunk(chunks - 1)

    def product(first_col, shift, values):
        return jnp.dot(
            az_w[first_col // run, :, shift * block:(shift + 1) * block], values,
            preferred_element_type=jnp.float32,
        )

    def focus(chunk, carry):
        for first_col in range(0, width, run):
            cols = slice(first_col, first_col + run)
            chosen = sets[chunk * width + first_col]
            for side in range(2):
                row = az_f32[side, pl.ds(chosen, 1), :]
                square = shifted_rows(row, block, (halo_blocks + 2) * block)
                az_w[first_col // run, side * block:(side + 1) * block, :] = (
                    square[:, :(halo_blocks + 1) * block].astype(jnp.bfloat16)
                )
            for part in range(own_blocks):
                for side in range(2):
                    sums[part, side, :, cols] = sum(
                        product(first_col, shift, comp[chunk, part + shift, side, :, cols])
                        for shift in range(min(halo_blocks + 1, own_blocks - part))
                    )

        for landed in range(-1, halo_blocks):
            if landed >= 0:
                @pl.when(az < az_size - 1)
                def _():
                    send(chunk, landed).wait_recv()

            for part in range(own_blocks):
                shift = own_blocks + landed - part
                last = shift == halo_blocks
                if landed < 0 and not last or shift > halo_blocks:
                    continue
                for first_col in range(0, width, run):
                    cols = slice(first_col, first_col + run)
                    total = [
                        sums[part, side, :, cols]
                        if landed < 0
                        else sums[part, side, :, cols]
                        + product(first_col, shift, halo[chunk, landed, side, :, cols])
                        for side in range(2)
                    ]
                    if last:
                        real, imag = total
                        rows = slice(part * block, (part + 1) * block)
                        start = pl.multiple_of(chunk * width + first_col, run)
                        out[0, rows, pl.ds(start, run)] = (
                            real[:block] + imag[block:]
                        ).astype(jnp.bfloat16)
                        out[1, rows, pl.ds(start, run)] = (
                            imag[:block] - real[block:]
                        ).astype(jnp.bfloat16)
                    else:
                        for side in range(2):
                            sums[part, side, :, cols] = total[side]
        return carry

    lax.fori_loop(0, chunks, focus, 0)

    @pl.when(rg > 0)
    def _():
        edge().wait_send()

    def finish(chunk, carry):
        for part in range(halo_blocks):
            @pl.when(az > 0)
            def _():
                send(chunk, part).wait_send()
        return carry

    lax.fori_loop(0, chunks, finish, 0)


def write_out(focused, out, sem):
    pieces = sem.shape[1]
    size = focused.shape[1] // pieces
    copies = [
        pltpu.make_async_copy(
            focused.at[side, piece * size:(piece + 1) * size],
            out.at[side, piece * size:(piece + 1) * size],
            sem.at[side, piece],
        )
        for side in range(2)
        for piece in range(pieces)
    ]
    for copy in copies:
        copy.start()
    for copy in copies:
        copy.wait()


def local(az_size, rg_size, raw, chirp, az_ref, set_index):
    _, lines, columns = raw.shape
    taps = chirp.shape[1]
    az_taps = az_ref.shape[2]
    width = taps
    chunks = columns // width
    run = min(columns // az_size, width)
    block = az_taps // 2
    own_blocks, halo_blocks = lines // block, az_taps // block
    assert columns % width == 0 and width % run == 0 and chunks > 1
    assert lines % block == 0 and own_blocks == halo_blocks
    tile = (2, block, width)
    focused = pl.pallas_call(
        functools.partial(kernel, az_size, rg_size, run),
        out_shape=pltpu.VMEM(raw.shape, jnp.bfloat16),
        in_specs=[pl.BlockSpec(memory_space=pl.ANY)] * 4,
        out_specs=pl.BlockSpec(memory_space=pltpu.VMEM),
        scratch_shapes=[
            pltpu.VMEM((chunks + 1, 2, lines, width), jnp.bfloat16),
            pltpu.VMEM((chunks, own_blocks) + tile, jnp.bfloat16),
            pltpu.VMEM((chunks, halo_blocks) + tile, jnp.bfloat16),
            pltpu.VMEM((width + taps, 2 * width), jnp.bfloat16),
            pltpu.VMEM((width // run, 2 * block, (halo_blocks + 1) * block), jnp.bfloat16),
            pltpu.VMEM((own_blocks, 2, 2 * block, width), jnp.float32),
            pltpu.VMEM(chirp.shape, chirp.dtype),
            pltpu.VMEM(az_ref.shape, az_ref.dtype),
            pltpu.VMEM(az_ref.shape, jnp.float32),
            pltpu.SMEM(set_index.shape, set_index.dtype),
            pltpu.SemaphoreType.DMA((chunks,)),
            pltpu.SemaphoreType.DMA((chunks, halo_blocks)),
            pltpu.SemaphoreType.DMA((chunks, halo_blocks)),
            pltpu.SemaphoreType.DMA((2,)),
            pltpu.SemaphoreType.DMA((3,)),
        ],
        compiler_params=pltpu.CompilerParams(
            collective_id=0, has_side_effects=True, vmem_limit_bytes=56 * 2**20
        ),
        cost_estimate=pl.CostEstimate(
            flops=11 * 10**9, bytes_accessed=4 * raw.size, transcendentals=0
        ),
    )(raw, chirp, az_ref, set_index)
    return pl.pallas_call(
        write_out,
        out_shape=jax.ShapeDtypeStruct(raw.shape, jnp.bfloat16),
        in_specs=[pl.BlockSpec(memory_space=pltpu.VMEM)],
        out_specs=pl.BlockSpec(memory_space=pl.ANY),
        scratch_shapes=[pltpu.SemaphoreType.DMA((2, lines // (block // 2)))],
        compiler_params=pltpu.CompilerParams(vmem_limit_bytes=16 * 2**20),
    )(focused)


def solution(mesh):
    in_specs = (P(None, "az", "rg"), P(), P(), P("rg"))
    out_specs = P(None, "az", "rg")
    body = functools.partial(local, mesh.shape["az"], mesh.shape["rg"])
    return jax.shard_map(body, mesh=mesh, in_specs=in_specs, out_specs=out_specs, check_vma=False)
```
